128 devices in a mesh: dp: 2 (over core), expert: 64 (over y, x, z).
Axes of the slice: x: 4, y: 4, z: 4, core: 2. Of those that a mesh axis runs over, the one named last changes fastest.
Arguments:
- tokens: bfloat16 [16384, 2048], P(('dp', 'expert')), may hold values from -6 to 6
- routes: int32 [16384, 8], P(('dp', 'expert')), may hold values from 0 to 63, all different within a row; in each aligned block of 128 rows (0 to 127, 128 to 255, ...) at most 18 rows name the same one
- router_weights: bfloat16 [16384, 8], P(('dp', 'expert')), may hold values from 0.019897461 to 0.5
- w_gate: bfloat16 [64, 2048, 768], P('expert'), may hold values from -0.125 to 0.125
- w_up: bfloat16 [64, 2048, 768], P('expert'), may hold values from -0.125 to 0.125
- w_down: bfloat16 [64, 768, 2048], P('expert'), may hold values from -0.21875 to 0.21875
- out_grad: bfloat16 [16384, 2048], P(('dp', 'expert')), may hold values from -1.5 to 1.5
Outputs:
- tokens_grad: bfloat16 [16384, 2048], P(('dp', 'expert'))
- router_grad: bfloat16 [16384, 8], P(('dp', 'expert'))
- w_gate_grad: bfloat16 [64, 2048, 768], P('expert', 'dp')
- w_up_grad: bfloat16 [64, 2048, 768], P('expert', 'dp')
- w_down_grad: bfloat16 [64, 768, 2048], P('expert', 'dp')
The draws below stay inside these ranges and needn't reach their ends.
Inputs may be any that keep to these rules, and one draw needn't show every extreme that they name: `routes`: each token names 8 different experts. Among the tokens of one device (aligned blocks of 128 tokens) no expert is named by more than 18 tokens, and some expert reaches 18 in some block of every draw.
All inputs are finite; a program needn't handle non-finite values.
Results may differ from the reference program's by a relative error of at most 0.015.
Values may be sent and summed in bfloat16 or wider, within the bound.
No kernel may reach another device: no remote copies, remote signals or barrier semaphores. Data moves between devices by JAX's collectives and lax.ppermute only.
A program may use at most 192 MiB of HBM per device.

```python
import math
import jax
import jax.numpy as jnp
import numpy as np
from jax import lax

D = 2048
FF = 768
TOPK = 8
TOK_DEV = 128
E = 64
MOST = 18
TOKENS = 16384


def levels(rng, dims, pieces, low, largest):
    factor_of = 1.0
    for axis_at, blocks in pieces:
        heights = jax.random.uniform(jax.random.fold_in(jax.random.fold_in(rng, 6), axis_at), (blocks,), jnp.float32, low / len(pieces), largest / len(pieces))
        factor_of = factor_of * jnp.repeat(jnp.exp(heights), dims[axis_at] // blocks).reshape((-1,) + (1,) * (len(dims) - 1 - axis_at))
    return factor_of


def shared_out(rng, own, number, rows, amount, top, limit, lean):
    sequence = jax.random.permutation(rng, amount)
    packed, ordinary = shares(amount, rows * top, limit, lean, True), shares(amount, rows * top, limit, lean, False)
    places = jnp.arange(amount)

    def named(lengths, rotation):
        used = int((lengths > 0).sum())
        fixed = max(1, used // 4)
        moved = fixed + (places - fixed + rotation * (used - fixed)) % max(1, amount - fixed)
        return jnp.zeros((amount,), jnp.int32).at[sequence[jnp.where(places < fixed, places, moved)]].set(jnp.asarray(lengths, jnp.int32))

    lengths = jnp.where(number % 4 == 0, named(packed, number // 4), named(ordinary, number - number // 4 - 1))
    mixed = jax.random.permutation(jax.random.fold_in(own, 3), amount)
    donor, taker = mixed[0:amount // 2 * 2:2], mixed[1:amount // 2 * 2:2]
    margin = jnp.minimum(lengths[donor] - 1, limit - lengths[taker]) // 2
    margin = jnp.where((donor == sequence[0]) | (taker == sequence[0]) | (lengths[taker] == 0), 0, jnp.maximum(margin, 0))
    moved = jax.random.randint(jax.random.fold_in(own, 4), (amount // 2,), 0, 1 << 20) % (margin + 1)
    lengths = lengths.at[donor].add(-moved).at[taker].add(moved)
    items = jnp.searchsorted(jnp.cumsum(lengths), jnp.arange(rows * top), side="right").astype(jnp.int32)
    table = items.reshape(top, rows).T
    table = table[jax.random.permutation(jax.random.fold_in(own, 1), rows)]
    rotation = jax.random.randint(jax.random.fold_in(own, 2), (rows, 1), 0, top)
    return jnp.take_along_axis(table, (jnp.arange(top)[None, :] + rotation) % top, axis=1)


def shares(amount, total, limit, lean, full):
    portions = [(1 << 20) // math.isqrt(standing ** lean) + 1 for standing in range(1, amount + 1)]
    largest = limit if full else min(limit, max(-(-total // amount), total * portions[0] // sum(portions)))
    least = 1 if total - largest >= amount - 1 else 0
    counts, spare = [largest] + [least] * (amount - 1), total - largest - least * (amount - 1)
    while spare > 0:
        movable = [i for i in range(1, amount) if counts[i] < largest] or [i for i in range(1, amount) if counts[i] < limit]
        pool, left = sum([portions[i] for i in movable]), spare
        for i in movable:
            more = min(limit - counts[i], max(1, left * portions[i] // pool), spare)
            counts[i] = counts[i] + more
            spare = spare - more
    return np.array(counts)


def scatter_about(own_key, shape, width, limit, pieces=(), held_as=jnp.bfloat16):
    entries = width * jax.random.normal(own_key, shape, jnp.float32)
    if pieces:
        entries = entries * levels(own_key, shape, pieces, -0.22, 0.18)
    return jnp.clip(entries, -limit, limit).astype(held_as)


def setup_inputs(seed: int = 0) -> dict:
    key_list = jax.random.split(jax.random.key(seed), 8)
    tokens = scatter_about(key_list[0], (TOKENS, D), 1.0, 6.0, ((0, 128),))
    routes_keys = jax.random.split(jax.random.fold_in(key_list[1], 1), TOKENS // TOK_DEV)
    routes_turns = jax.random.permutation(jax.random.fold_in(key_list[1], 3), TOKENS // TOK_DEV)
    routes = jax.vmap(lambda own, number: shared_out(jax.random.fold_in(key_list[1], 2), own, number, TOK_DEV, E, TOPK, MOST, 2))(routes_keys, routes_turns).reshape((TOKENS, TOPK))
    router_weights = jnp.clip(jnp.exp(math.log(0.5) - 3.224016 * jax.random.uniform(key_list[2], (TOKENS, TOPK), jnp.float32) ** levels(key_list[2], (TOKENS, TOPK), ((0, 128),), -0.2, 0.2)), 0.019897461, 0.5).astype(jnp.bfloat16)
    w_gate = scatter_about(key_list[3], (E, D, FF), D ** -0.5, 0.125, ((0, 64),))
    w_up = scatter_about(key_list[4], (E, D, FF), D ** -0.5, 0.125, ((0, 64),))
    w_down = scatter_about(key_list[5], (E, FF, D), FF ** -0.5, 0.21875, ((0, 64),))
    out_grad = scatter_about(key_list[6], (TOKENS, D), 0.25, 1.5, ((0, 128),))
    return {"tokens": tokens, "routes": routes, "router_weights": router_weights, "w_gate": w_gate, "w_up": w_up, "w_down": w_down, "out_grad": out_grad}


def reference(tokens, routes, router_weights, w_gate, w_up, w_down, out_grad):
    experts_all = w_gate.shape[0]
    flat_experts = routes.reshape(-1).astype(jnp.int32)
    row_total = flat_experts.shape[0]
    spare = MOST * (TOKENS // TOK_DEV)
    counted = jnp.sum((flat_experts[:, None] == jnp.arange(experts_all, dtype=jnp.int32)[None, :]).astype(jnp.int32), axis=0)
    offsets = (jnp.cumsum(counted) - counted).astype(jnp.int32)
    sorted_rows = jnp.argsort(flat_experts, stable=True).astype(jnp.int32)
    padded_rows = jnp.concatenate([sorted_rows, jnp.zeros((spare,), jnp.int32)])
    flat_weights = router_weights.reshape(-1)
    positions = jnp.arange(spare, dtype=jnp.int32)

    def one_expert(carry, inputs):
        token_acc, router_acc = carry
        gate_w, up_w, down_w, expert_id = inputs
        chosen_rows = lax.dynamic_slice(padded_rows, (offsets[expert_id],), (spare,)).astype(jnp.int32)
        valid_row = (positions < counted[expert_id]).astype(jnp.float32)
        valid = valid_row[:, None]
        token_ids = (chosen_rows // TOPK).astype(jnp.int32)
        rows_x = jnp.take(tokens, token_ids, axis=0)
        rows_dy = jnp.take(out_grad, token_ids, axis=0)
        weight = jnp.take(flat_weights, chosen_rows).astype(jnp.float32)[:, None] * valid
        pre_gate = jnp.dot(rows_x, gate_w, preferred_element_type=jnp.float32)
        pre_up = jnp.dot(rows_x, up_w, preferred_element_type=jnp.float32)
        sigmoid_gate = jax.nn.sigmoid(pre_gate)
        active = pre_gate * sigmoid_gate
        hidden = active * pre_up
        back_hidden = lax.dot_general(rows_dy, down_w, (((1,), (1,)), ((), ())), preferred_element_type=jnp.float32)
        router_part = jnp.sum(back_hidden * hidden, axis=1).astype(jnp.bfloat16)
        scaled_back = weight * back_hidden
        grad_gate = (scaled_back * pre_up * sigmoid_gate * (1.0 + pre_gate * (1.0 - sigmoid_gate))).astype(jnp.bfloat16)
        grad_up = (scaled_back * active).astype(jnp.bfloat16)
        scaled_hidden = (weight * hidden).astype(jnp.bfloat16)
        token_part = lax.dot_general(grad_gate, gate_w, (((1,), (1,)), ((), ())), preferred_element_type=jnp.float32)
        token_part = token_part + lax.dot_general(grad_up, up_w, (((1,), (1,)), ((), ())), preferred_element_type=jnp.float32)
        token_part = token_part.astype(jnp.bfloat16)
        token_acc = token_acc.at[token_ids].add(token_part.astype(jnp.float32) * valid)
        router_acc = router_acc.at[chosen_rows].add(router_part.astype(jnp.float32) * valid_row)
        gate_grad = lax.dot_general(rows_x, grad_gate, (((0,), (0,)), ((), ())), preferred_element_type=jnp.float32).astype(jnp.bfloat16)
        up_grad = lax.dot_general(rows_x, grad_up, (((0,), (0,)), ((), ())), preferred_element_type=jnp.float32).astype(jnp.bfloat16)
        down_grad = lax.dot_general(scaled_hidden, rows_dy, (((0,), (0,)), ((), ())), preferred_element_type=jnp.float32).astype(jnp.bfloat16)
        return (token_acc, router_acc), (gate_grad, up_grad, down_grad)

    start_carry = (jnp.zeros(tokens.shape, jnp.float32), jnp.zeros((row_total,), jnp.float32))
    expert_ids = jnp.arange(experts_all, dtype=jnp.int32)
    (token_acc, router_acc), (gate_grads, up_grads, down_grads) = lax.scan(one_expert, start_carry, (w_gate, w_up, w_down, expert_ids))
    tokens_grad = token_acc.astype(jnp.bfloat16)
    router_grad = router_acc.reshape(routes.shape).astype(jnp.bfloat16)
    return (tokens_grad, router_grad, gate_grads, up_grads, down_grads)
```

```python
import functools

import jax
import jax.numpy as jnp
from jax import lax
from jax.experimental import pallas as pl
from jax.experimental.pallas import tpu as pltpu
from jax.sharding import PartitionSpec as P

F32, BF16 = jnp.float32, jnp.bfloat16
SLOTS = 16
EXTRA = 2
GROUP = 16
ROWS = GROUP * (SLOTS + EXTRA)
MAIN = GROUP * SLOTS
LANES = 128
MIB = 1 << 20


def iota(shape, axis):
    return lax.broadcasted_iota(jnp.int32, shape, axis)


def dot(a, b):
    return jnp.dot(a, b, preferred_element_type=F32)


def dot_rows(a, b):
    return lax.dot_general(a, b, (((0,), (0,)), ((), ())), preferred_element_type=F32)


def unit(n, m):
    return (iota((n, m), 0) == iota((n, m), 1)).astype(BF16)


def spread_rows(block):
    wide = jnp.broadcast_to(block[:, None, :], (GROUP, 16, LANES))
    return wide.reshape(MAIN, LANES)


def chunk_rows(value, pieces):
    width = value.shape[1] // pieces
    return jnp.concatenate([value[:, i * width : (i + 1) * width] for i in range(pieces)], axis=0)


def chunk_columns(value, pieces):
    height = value.shape[0] // pieces
    return jnp.concatenate([value[i * height : (i + 1) * height] for i in range(pieces)], axis=1)


def tile_rows(ref, blocks):
    return jnp.concatenate(
        [ref[:, j * 16 : (j + 1) * 16, :].reshape(MAIN, LANES) for j in blocks], axis=1
    )


def put_tiles(ref, value, first):
    for j in range(value.shape[1] // LANES):
        at = (first + j) * 16
        ref[:, at : at + 16, :] = value[:, j * LANES : (j + 1) * LANES].reshape(GROUP, 16, LANES)


def route_tables(routes_ref, weights_ref, rank_ref, weight_ref):
    tokens = routes_ref.shape[0]
    experts = iota((tokens, LANES), 1)
    mask = jnp.zeros((tokens, LANES), F32)
    weight = jnp.zeros((tokens, LANES), F32)
    for k in range(routes_ref.shape[1]):
        hit = routes_ref[:, k : k + 1] == experts
        mask = mask + hit.astype(F32)
        if weights_ref is not None:
            weight = weight + jnp.where(hit, weights_ref[:, k : k + 1].astype(F32), 0.0)
    mask = mask.astype(BF16)
    earlier = (iota((tokens, tokens), 0) < iota((tokens, tokens), 1)).astype(BF16)
    same = unit(tokens, tokens)
    rank = dot_rows(mask, earlier)
    rank_ref[...] = jnp.where(dot_rows(mask, same) > 0.5, rank, -1.0)
    if weights_ref is not None:
        weight_ref[...] = dot_rows(weight.astype(BF16), same)


def slot_masks(ranks):
    wide = spread_rows(ranks)
    place = iota((MAIN, LANES), 0) % 16
    main = wide == place.astype(F32)
    over = wide == (SLOTS + place // 8).astype(F32)
    return wide, place, main, over


def over_pieces(over, place):
    return jnp.concatenate(
        [jnp.where(over & (place % 8 == c), 1.0, 0.0).astype(BF16) for c in range(8)], axis=1
    )


def pack_kernel(scalars, routes_ref, weights_ref, rows_ref, send_ref, *rest):
    rank_out = None if scalars else rest[0]
    rank_ref, weight_ref = rest[-2:]
    step = pl.program_id(0)

    @pl.when(step == 0)
    def _():
        route_tables(routes_ref, weights_ref if scalars else None, rank_ref, weight_ref)

    here = pl.ds(pl.multiple_of(step * GROUP, GROUP), GROUP)
    ranks = rank_ref[here, :]
    wide, place, main, over = slot_masks(ranks)
    rows = rows_ref[...]
    put_tiles(send_ref, dot(main.astype(F32).astype(BF16), rows).astype(BF16), 0)
    put_tiles(send_ref, dot(over_pieces(over, place), chunk_rows(rows, 8)).astype(BF16), 16)
    if scalars:
        weight = spread_rows(weight_ref[here, :])
        first = jnp.where(main, weight, 0.0).astype(BF16)
        second = jnp.where(wide == (SLOTS + place).astype(F32), weight, 0.0).astype(BF16)
        low = (iota((LANES, LANES), 1) < 64).astype(F32)
        tile = dot(first, low.astype(BF16)) + dot(second, (1.0 - low).astype(BF16))
        put_tiles(send_ref, tile.astype(BF16), 18)
    else:
        rank_out[...] = ranks


def over_select():
    shape = (8 * EXTRA * GROUP, MAIN)
    row, col = iota(shape, 0), iota(shape, 1)
    c, r, s = row // (EXTRA * GROUP), (row // GROUP) % EXTRA, row % GROUP
    return (col == s * 16 + r * 8 + c).astype(F32).astype(BF16)


def unpack(recv_ref):
    main = tile_rows(recv_ref, range(16))
    pieces = dot(over_select(), tile_rows(recv_ref, (16, 17))).astype(BF16)
    return jnp.concatenate([main, chunk_columns(pieces, 8)], axis=0)


def forward_kernel(recv_ref, gate_ref, up_ref, x_ref, act_ref, slope_ref, hidden_ref):
    x = unpack(recv_ref)
    x_ref[...] = x
    pre_gate = dot(x, gate_ref[...])
    pre_up = dot(x, up_ref[...])
    sig = jax.nn.sigmoid(pre_gate)
    active = pre_gate * sig
    act_ref[...] = active
    slope_ref[...] = pre_up * sig * (1.0 + pre_gate * (1.0 - sig))
    hidden_ref[...] = active * pre_up


def backward_kernel(
    recv_ref,
    act_ref,
    slope_ref,
    hidden_ref,
    down_ref,
    both_ref,
    send_ref,
    dy_ref,
    gate_grads_ref,
    up_grads_ref,
    sh_ref,
):
    dy = unpack(recv_ref)
    dy_ref[...] = dy
    tile = tile_rows(recv_ref, (18,))
    shape = (EXTRA * GROUP, MAIN)
    row = iota(shape, 0)
    pick = (iota(shape, 1) == (row % GROUP) * 16 + row // GROUP).astype(F32).astype(BF16)
    weight = jnp.concatenate(
        [tile[:, 0:1].astype(F32), dot(pick, tile)[:, 64:65]], axis=0
    )
    back = dot(dy, down_ref[...])
    hidden = hidden_ref[...]
    router = jnp.sum(back * hidden, axis=1, keepdims=True)
    scaled = weight * back
    sh_ref[...] = (weight * hidden).astype(BF16)
    gate_grads = (scaled * slope_ref[...]).astype(BF16)
    up_grads = (scaled * act_ref[...]).astype(BF16)
    gate_grads_ref[...] = gate_grads
    up_grads_ref[...] = up_grads
    grads = jnp.concatenate([gate_grads, up_grads], axis=1)
    part = dot(grads, both_ref[...]).astype(BF16)
    put_tiles(send_ref, part[:MAIN], 0)
    pieces = chunk_rows(part[MAIN:], 8)
    put_tiles(send_ref, dot_rows(over_select(), pieces).astype(BF16), 16)
    router_wide = jnp.broadcast_to(router, (ROWS, LANES))
    second = dot_rows(pick, router_wide[MAIN:].astype(BF16))
    lane = iota((MAIN, LANES), 1)
    put_tiles(send_ref, jnp.where(lane < 64, router_wide[:MAIN], second).astype(BF16), 18)


def combine_kernel(recv_ref, rank_ref, routes_ref, grad_ref, router_ref, total_ref, value_ref):
    step = pl.program_id(0)
    tokens = routes_ref.shape[0]

    @pl.when(step == 0)
    def _():
        total_ref[...] = jnp.zeros_like(total_ref)

    wide, place, main, over = slot_masks(rank_ref[...])
    total_ref[...] += dot_rows(main.astype(F32).astype(BF16), tile_rows(recv_ref, range(16)))
    pieces = dot_rows(over_pieces(over, place), tile_rows(recv_ref, (16, 17)))
    total_ref[...] += chunk_columns(pieces, 8)
    tile = tile_rows(recv_ref, (18,)).astype(F32)
    value = jnp.where(main, tile[:, 0:1], 0.0) + jnp.where(
        wide == (SLOTS + place).astype(F32), tile[:, 64:65], 0.0
    )
    here = pl.ds(pl.multiple_of(step * GROUP, GROUP), GROUP)
    value_ref[here, :] = jnp.sum(value.reshape(GROUP, 16, LANES), axis=1)

    @pl.when(step == pl.num_programs(0) - 1)
    def _():
        grad_ref[...] = total_ref[...].astype(BF16)
        by_token = dot_rows(value_ref[...].astype(BF16), unit(value_ref.shape[0], LANES))
        experts = iota((tokens, LANES), 1)
        lane = iota(router_ref.shape, 1)
        out = jnp.zeros(router_ref.shape, F32)
        for k in range(router_ref.shape[1]):
            picked = jnp.where(routes_ref[:, k : k + 1] == experts, by_token, 0.0)
            out = jnp.where(lane == k, jnp.sum(picked, axis=1, keepdims=True), out)
        router_ref[...] = out.astype(BF16)


def whole(shape):
    return pl.BlockSpec(shape, lambda i: (0,) * len(shape), pipeline_mode=pl.Buffered(1))


def params(mib):
    return pltpu.CompilerParams(
        vmem_limit_bytes=mib * MIB, dimension_semantics=("arbitrary",)
    )


def cost(flops, size):
    return pl.CostEstimate(flops=flops, bytes_accessed=size, transcendentals=0)


def pack(scalars, experts, routes, weights, rows):
    tokens, width = rows.shape
    high = 16 * (width // LANES) + 32 + 16 * scalars
    outs = [jax.ShapeDtypeStruct((experts, high, LANES), BF16)]
    out_specs = [pl.BlockSpec((GROUP, high, LANES), lambda i: (i, 0, 0))]
    if not scalars:
        outs.append(jax.ShapeDtypeStruct((experts, tokens), F32))
        out_specs.append(pl.BlockSpec((GROUP, tokens), lambda i: (i, 0)))
    return pl.pallas_call(
        functools.partial(pack_kernel, scalars),
        grid=(experts // GROUP,),
        in_specs=[whole(routes.shape), whole(weights.shape), whole(rows.shape)],
        out_specs=out_specs,
        out_shape=outs,
        scratch_shapes=[pltpu.VMEM((LANES, tokens), F32)] * 2,
        compiler_params=params(32),
        cost_estimate=cost(4 * experts * 18 * tokens * width, 2 * experts * high * LANES),
        name="pack_rows",
    )(routes, weights, rows)


def forward(recv, gate, up):
    sources, high, _ = recv.shape
    width, units = gate.shape
    total = sources * (SLOTS + EXTRA)
    by_rows = lambda n: pl.BlockSpec((ROWS, n), lambda i: (i, 0))
    return pl.pallas_call(
        forward_kernel,
        grid=(sources // GROUP,),
        in_specs=[
            pl.BlockSpec((GROUP, high, LANES), lambda i: (i, 0, 0)),
            whole(gate.shape),
            whole(up.shape),
        ],
        out_specs=[by_rows(width), by_rows(units), by_rows(units), by_rows(units)],
        out_shape=[
            jax.ShapeDtypeStruct((total, width), BF16),
            jax.ShapeDtypeStruct((total, units), F32),
            jax.ShapeDtypeStruct((total, units), F32),
            jax.ShapeDtypeStruct((total, units), F32),
        ],
        compiler_params=params(48),
        cost_estimate=cost(4 * total * width * units, 30 * MIB),
        name="expert_forward",
    )(recv, gate, up)


def backward(recv, act, slope, hidden, down, both):
    sources, high, _ = recv.shape
    width, units = down.shape
    total = sources * (SLOTS + EXTRA)
    by_rows = lambda n: pl.BlockSpec((ROWS, n), lambda i: (i, 0))
    by_source = pl.BlockSpec((GROUP, high, LANES), lambda i: (i, 0, 0))
    return pl.pallas_call(
        backward_kernel,
        grid=(sources // GROUP,),
        in_specs=[
            by_source,
            by_rows(units),
            by_rows(units),
            by_rows(units),
            whole(down.shape),
            whole(both.shape),
        ],
        out_specs=[by_source, by_rows(width), by_rows(units), by_rows(units), by_rows(units)],
        out_shape=[
            jax.ShapeDtypeStruct(recv.shape, BF16),
            jax.ShapeDtypeStruct((total, width), BF16),
            jax.ShapeDtypeStruct((total, units), BF16),
            jax.ShapeDtypeStruct((total, units), BF16),
            jax.ShapeDtypeStruct((total, units), BF16),
        ],
        compiler_params=params(48),
        cost_estimate=cost(6 * total * width * units, 40 * MIB),
        name="expert_backward",
    )(recv, act, slope, hidden, down, both)


def combine(recv, ranks, routes, width):
    experts, high, _ = recv.shape
    tokens, chosen = routes.shape
    return pl.pallas_call(
        combine_kernel,
        grid=(experts // GROUP,),
        in_specs=[
            pl.BlockSpec((GROUP, high, LANES), lambda i: (i, 0, 0)),
            pl.BlockSpec((GROUP, tokens), lambda i: (i, 0)),
            whole(routes.shape),
        ],
        out_specs=[
            pl.BlockSpec((tokens, width), lambda i: (0, 0)),
            pl.BlockSpec((tokens, chosen), lambda i: (0, 0)),
        ],
        out_shape=[
            jax.ShapeDtypeStruct((tokens, width), BF16),
            jax.ShapeDtypeStruct((tokens, chosen), BF16),
        ],
        scratch_shapes=[pltpu.VMEM((tokens, width), F32), pltpu.VMEM((experts, tokens), F32)],
        compiler_params=params(32),
        cost_estimate=cost(4 * experts * 18 * tokens * width, 2 * experts * high * LANES),
        name="combine_parts",
    )(recv, ranks, routes)


def exchange(value):
    return lax.all_to_all(value, "expert", split_axis=0, concat_axis=0, tiled=True)


def summed_halves(left, right):
    half = left.shape[1] // 2
    me = lax.axis_index("dp")
    theirs = lax.dynamic_slice_in_dim(left, (1 - me) * half, half, axis=1)
    mine = lax.dynamic_slice_in_dim(left, me * half, half, axis=1)
    arrived = lax.ppermute(dot_rows(theirs, right).astype(BF16), "dp", [(0, 1), (1, 0)])
    return (dot_rows(mine, right) + arrived.astype(F32)).astype(BF16)


def body(tokens, routes, router_weights, w_gate, w_up, w_down, out_grad):
    experts = lax.axis_size("expert")
    width = tokens.shape[1]
    gate, up, down = w_gate[0], w_up[0], w_down[0]
    units = gate.shape[1]
    send_x, ranks = pack(False, experts, routes, router_weights, tokens)
    recv_x = exchange(send_x)
    _, routes_b, out_grad, gate_b, up_b, down_b = lax.optimization_barrier(
        (ranks, routes, out_grad, gate, up, down)
    )
    send_dy = pack(True, experts, routes_b, router_weights, out_grad)[0]
    both = jnp.concatenate([gate_b.T, up_b.T], axis=0)
    down_t = down_b.T
    recv_dy = exchange(send_dy)
    x, act, slope, hidden = forward(recv_x, gate, up)
    send_back, dy, gate_grads, up_grads, scaled_hidden = backward(recv_dy, act, slope, hidden, down_t, both)
    recv_back = exchange(send_back)
    gate_grad = summed_halves(x, gate_grads)
    up_grad = summed_halves(x, up_grads)
    down_grad = summed_halves(scaled_hidden, dy)
    tokens_grad, router_grad = combine(recv_back, ranks, routes, width)
    return (
        tokens_grad,
        router_grad,
        gate_grad[None],
        up_grad[None],
        down_grad[None],
    )


def solution(mesh):
    placed = (
        P(("dp", "expert"), None),
        P(("dp", "expert"), None),
        P(("dp", "expert"), None),
        P("expert", None, None),
        P("expert", None, None),
        P("expert", None, None),
        P(("dp", "expert"), None),
    )
    return jax.shard_map(
        body,
        mesh=mesh,
        in_specs=placed,
        out_specs=(
            P(("dp", "expert"), None),
            P(("dp", "expert"), None),
            P("expert", "dp", None),
            P("expert", "dp", None),
            P("expert", "dp", None),
        ),
        check_vma=False,
    )
```

```python
import functools

import jax
import jax.numpy as jnp
from jax import lax
from jax.experimental import pallas as pl
from jax.experimental.pallas import tpu as pltpu
from jax.sharding import PartitionSpec as P

F32, BF16 = jnp.float32, jnp.bfloat16
PARTS = 2
SLOTS = 8
GROUP = 16
MAIN = GROUP * SLOTS
ROWS = MAIN + GROUP
FINE = GROUP * 16
TILES = 9
STEP = 2
LANES = 128
MIB = 1 << 20


def iota(shape, axis):
    return lax.broadcasted_iota(jnp.int32, shape, axis)


def dot(a, b):
    return jnp.dot(a, b, preferred_element_type=F32)


def dot_columns(a, b):
    return lax.dot_general(a, b, (((1,), (1,)), ((), ())), preferred_element_type=F32)


def dot_rows(a, b):
    return lax.dot_general(a, b, (((0,), (0,)), ((), ())), preferred_element_type=F32)


def ones_where(mask):
    return jnp.where(mask, 1.0, 0.0).astype(BF16)


def unit(n, m):
    return ones_where(iota((n, m), 0) == iota((n, m), 1))


def spread_rows(block):
    wide = jnp.broadcast_to(block[:, None, :], (GROUP, 16, LANES))
    return wide.reshape(FINE, LANES)


def chunk_rows(value, pieces):
    width = value.shape[1] // pieces
    return jnp.concatenate([value[:, i * width : (i + 1) * width] for i in range(pieces)], axis=0)


def chunk_columns(value, pieces):
    height = value.shape[0] // pieces
    return jnp.concatenate([value[i * height : (i + 1) * height] for i in range(pieces)], axis=1)


def get_tiles(ref, group, first, count):
    here = slice(group * GROUP, (group + 1) * GROUP)
    return jnp.concatenate(
        [
            ref[here, j * 16 : (j + 1) * 16, :].reshape(FINE, LANES)
            for j in range(first, first + count)
        ],
        axis=1,
    )


def put_tiles(ref, group, first, value):
    here = slice(group * GROUP, (group + 1) * GROUP)
    for j in range(value.shape[1] // LANES):
        at = (first + j) * 16
        ref[here, at : at + 16, :] = value[:, j * LANES : (j + 1) * LANES].reshape(
            GROUP, 16, LANES
        )


def fine_of(pieces):
    row, col = iota((FINE, FINE), 0), iota((FINE, FINE), 1)
    s, q = row // 16, row % 16
    rows = 16 // pieces
    return ones_where(col == (q % pieces) * (FINE // pieces) + s * rows + q // pieces)


def rows_of(pieces):
    row, col = iota((FINE, FINE), 0), iota((FINE, FINE), 1)
    rows = 16 // pieces
    c, s, r = row // (FINE // pieces), (row // rows) % GROUP, row % rows
    return ones_where(col == s * 16 + r * pieces + c)


def unpack(ref, group, first):
    main = dot(rows_of(2), get_tiles(ref, group, first, TILES - 1)).astype(BF16)
    last = dot(rows_of(16), get_tiles(ref, group, first + TILES - 1, 1)).astype(BF16)
    return jnp.concatenate([chunk_columns(main, 2), chunk_columns(last, 16)], axis=0)


def repack(ref, group, first, rows):
    main = dot(fine_of(2), chunk_rows(rows[:MAIN], 2)).astype(BF16)
    last = dot(fine_of(16), chunk_rows(rows[MAIN:], 16)).astype(BF16)
    put_tiles(ref, group, first, main)
    put_tiles(ref, group, first + TILES - 1, last)


def route_tables(routes_ref, weights_ref, experts):
    chosen, tokens = routes_ref.shape
    expert = iota((experts, tokens), 0)
    mask = jnp.zeros((experts, tokens), F32)
    weight = jnp.zeros((experts, tokens), F32)
    for k in range(chosen):
        hit = routes_ref[k : k + 1, :] == expert
        mask = mask + jnp.where(hit, 1.0, 0.0)
        weight = weight + jnp.where(hit, weights_ref[k : k + 1, :].astype(F32), 0.0)
    earlier = ones_where(iota((tokens, tokens), 0) < iota((tokens, tokens), 1))
    return jnp.where(mask > 0.5, dot(mask.astype(BF16), earlier), -1.0), weight


def pack_kernel(part, routes_ref, weights_ref, x_ref, dy_ref, send_ref, ranks_ref, rank_ref, weight_ref):
    step = pl.program_id(0)

    @pl.when(step == 0)
    def _():
        rank_ref[...], weight_ref[...] = route_tables(routes_ref, weights_ref, rank_ref.shape[0])

    here = pl.ds(pl.multiple_of(step * GROUP, GROUP), GROUP)
    ranks_ref[...] = rank_ref[here, :]
    ranks, weights = rank_ref[here, :], weight_ref[here, :]
    wide, weight = spread_rows(ranks), spread_rows(weights)
    fine = iota((FINE, LANES), 0) % 16
    main = wide == (part * SLOTS + fine // 2).astype(F32)
    over = ranks == float(PARTS * SLOTS + part)
    for first, ref, value, single in ((0, x_ref, 1.0, 1.0), (TILES, dy_ref, weight, weights)):
        rows = ref[...]
        pick = jnp.concatenate(
            [jnp.where(main & (fine % 2 == c), value, 0.0).astype(BF16) for c in range(2)], axis=1
        )
        put_tiles(send_ref, 0, first, dot(pick, chunk_rows(rows, 2)).astype(BF16))
        last = dot(jnp.where(over, single, 0.0).astype(BF16), rows).astype(BF16)
        piece = dot(fine_of(16), chunk_rows(last, 16))
        put_tiles(send_ref, 0, first + TILES - 1, piece.astype(BF16))


def expert_kernel(part, recv_ref, gate_ref, up_ref, down_ref, *refs):
    outs = refs[-6:-1] if part == 0 else refs[-5:]
    send_ref, x_ref, dy_ref, grads_ref, sh_ref = outs
    units = gate_ref.shape[1]
    x = jnp.concatenate([unpack(recv_ref, i, 0) for i in range(STEP)], axis=0)
    dy = jnp.concatenate([unpack(recv_ref, i, TILES) for i in range(STEP)], axis=0)
    x_ref[...] = x
    dy_ref[...] = dy
    pre_gate = dot(x, gate_ref[...])
    pre_up = dot(x, up_ref[...])
    back = dot_columns(dy, down_ref[...])
    sig = jax.nn.sigmoid(pre_gate)
    active = pre_gate * sig
    hidden = active * pre_up
    sh_ref[...] = hidden.astype(BF16)
    router = jnp.sum(back * hidden, axis=1, keepdims=True)
    gate_grads = (back * pre_up * sig * (1.0 + pre_gate * (1.0 - sig))).astype(BF16)
    up_grads = (back * active).astype(BF16)
    grads_ref[:, :units] = gate_grads
    grads_ref[:, units:] = up_grads
    token_part = dot_columns(gate_grads, gate_ref[...]) + dot_columns(up_grads, up_ref[...])
    token_part = token_part.astype(BF16)
    router = jnp.broadcast_to(router, (STEP * ROWS, LANES)).astype(BF16)
    if part == 0:
        refs[-1][...] = router
    for i in range(STEP):
        rows = slice(i * ROWS, (i + 1) * ROWS)
        repack(send_ref, i, 0, token_part[rows])
        if part == 1:
            both_parts = jnp.concatenate([refs[0][rows, :], router[rows]], axis=0)
            shape = (FINE, PARTS * ROWS)
            fine, col = iota(shape, 0), iota(shape, 1)
            s, q = fine // 16, fine % 16
            main = ones_where(col == (q // SLOTS) * ROWS + s * SLOTS + q % SLOTS)
            over = ones_where((q < PARTS) & (col == q * ROWS + MAIN + s))
            low = iota((FINE, LANES), 1) < LANES // 2
            tile = jnp.where(low, dot(main, both_parts), dot(over, both_parts))
            put_tiles(send_ref, i, TILES, tile.astype(BF16))


def add_rows(part, ref, ranks, total_ref):
    tokens = ranks.shape[1]
    across = ones_where(iota((GROUP, FINE), 0) == iota((GROUP, FINE), 1) // 16)
    by_token = dot_rows(ranks.astype(BF16), across)
    single = dot_rows(ranks.astype(BF16), unit(GROUP, GROUP))
    fine = iota((tokens, FINE), 1) % 16
    main = by_token == (part * SLOTS + fine // 2).astype(F32)
    tiles = get_tiles(ref, 0, 0, TILES - 1)
    half = [dot(ones_where(main & (fine % 2 == c)), tiles) for c in range(2)]
    last = dot(rows_of(16), get_tiles(ref, 0, TILES - 1, 1)).astype(BF16)
    over = ones_where(single == float(PARTS * SLOTS + part))
    total_ref[...] += jnp.concatenate(half, axis=1) + dot(over, chunk_columns(last, 16))


def first_sum_kernel(recv_ref, rank_ref, total_ref):
    @pl.when(pl.program_id(0) == 0)
    def _():
        total_ref[...] = jnp.zeros_like(total_ref)

    add_rows(0, recv_ref, rank_ref[...], total_ref)


def combine_kernel(
    recv_ref, rank_ref, first_ref, routes_ref, weights_ref, grad_ref, router_ref, total_ref, value_ref
):
    step = pl.program_id(0)
    chosen, tokens = routes_ref.shape

    @pl.when(step == 0)
    def _():
        total_ref[...] = first_ref[...]

    ranks = rank_ref[...]
    add_rows(1, recv_ref, ranks, total_ref)
    wide = spread_rows(ranks)
    place = iota((FINE, LANES), 0) % 16
    tile = get_tiles(recv_ref, 0, TILES, 1).astype(F32)
    middle = LANES // 2
    value = jnp.where(wide == place.astype(F32), tile[:, 0:1], 0.0) + jnp.where(
        wide == (PARTS * SLOTS + place).astype(F32), tile[:, middle : middle + 1], 0.0
    )
    here = pl.ds(pl.multiple_of(step * GROUP, GROUP), GROUP)
    value_ref[here, :] = jnp.sum(value.reshape(GROUP, 16, LANES), axis=1)

    @pl.when(step == pl.num_programs(0) - 1)
    def _():
        grad_ref[...] = total_ref[...].astype(BF16)
        expert = iota(value_ref.shape, 0)
        row = iota((chosen, tokens), 0)
        out = jnp.zeros((chosen, tokens), F32)
        for k in range(chosen):
            picked = jnp.where(routes_ref[k : k + 1, :] == expert, value_ref[...], 0.0)
            out = jnp.where(row == k, jnp.sum(picked, axis=0, keepdims=True), out)
        router_ref[...] = (out / weights_ref[...].astype(F32)).astype(BF16)


def whole(shape):
    return pl.BlockSpec(shape, lambda i: (0,) * len(shape), pipeline_mode=pl.Buffered(1))


def params(mib):
    return pltpu.CompilerParams(vmem_limit_bytes=mib * MIB, dimension_semantics=("arbitrary",))


def cost(flops, size):
    return pl.CostEstimate(flops=flops, bytes_accessed=size, transcendentals=0)


def by_group(size, high):
    return pl.BlockSpec((size, high, LANES), lambda i: (i, 0, 0))


def pack(part, experts, routes, weights, x, dy):
    tokens, width = x.shape
    high = 2 * TILES * 16
    return pl.pallas_call(
        functools.partial(pack_kernel, part),
        grid=(experts // GROUP,),
        in_specs=[whole(routes.shape), whole(weights.shape), whole(x.shape), whole(dy.shape)],
        out_specs=[by_group(GROUP, high), pl.BlockSpec((GROUP, tokens), lambda i: (i, 0))],
        out_shape=[
            jax.ShapeDtypeStruct((experts, high, LANES), BF16),
            jax.ShapeDtypeStruct((experts, tokens), F32),
        ],
        scratch_shapes=[pltpu.VMEM((experts, tokens), F32)] * 2,
        compiler_params=params(60),
        cost_estimate=cost(8 * experts * 16 * tokens * width, 2 * experts * high * LANES),
        name="pack_rows",
    )(routes, weights, x, dy)


def expert(part, recv, gate, up, down, held=()):
    sources = recv.shape[0]
    width, units = gate.shape
    rows = sources // GROUP * ROWS
    steps = sources // (STEP * GROUP)
    high = (TILES + part) * 16
    by_rows = lambda n: pl.BlockSpec((STEP * ROWS, n), lambda i: (i + part * steps, 0))
    router = pl.BlockSpec((STEP * ROWS, LANES), lambda i: (i, 0))
    anywhere = pl.BlockSpec(memory_space=pl.ANY)
    return pl.pallas_call(
        functools.partial(expert_kernel, part),
        grid=(steps,),
        in_specs=[by_group(STEP * GROUP, recv.shape[1])]
        + [whole(w.shape) for w in (gate, up, down)]
        + ([router] + [anywhere] * 4 if part else []),
        out_specs=[by_group(STEP * GROUP, high)]
        + [by_rows(n) for n in (width, width, 2 * units, units)]
        + ([] if part else [router]),
        out_shape=[jax.ShapeDtypeStruct((sources, high, LANES), BF16)]
        + [
            jax.ShapeDtypeStruct((PARTS * rows, n), BF16) for n in (width, width, 2 * units, units)
        ]
        + ([] if part else [jax.ShapeDtypeStruct((rows, LANES), BF16)]),
        input_output_aliases={5 + i: 1 + i for i in range(4)} if part else {},
        compiler_params=params(60),
        cost_estimate=cost(10 * rows * width * units, 30 * MIB),
        name="expert",
    )(recv, gate, up, down, *held)


def first_sum(recv, ranks, width):
    experts, tokens = ranks.shape
    return pl.pallas_call(
        first_sum_kernel,
        grid=(experts // GROUP,),
        in_specs=[
            by_group(GROUP, recv.shape[1]),
            pl.BlockSpec((GROUP, tokens), lambda i: (i, 0)),
        ],
        out_specs=pl.BlockSpec((tokens, width), lambda i: (0, 0)),
        out_shape=jax.ShapeDtypeStruct((tokens, width), F32),
        compiler_params=params(32),
        cost_estimate=cost(4 * experts * 9 * tokens * width, 4 * experts * 80 * LANES),
        name="first_sum",
    )(recv, ranks)


def combine(recv, ranks, first, routes, weights):
    experts = recv.shape[0]
    chosen, tokens = routes.shape
    width = first.shape[1]
    return pl.pallas_call(
        combine_kernel,
        grid=(experts // GROUP,),
        in_specs=[
            by_group(GROUP, recv.shape[1]),
            pl.BlockSpec((GROUP, tokens), lambda i: (i, 0)),
            whole(first.shape),
            whole(routes.shape),
            whole(weights.shape),
        ],
        out_specs=[
            pl.BlockSpec((tokens, width), lambda i: (0, 0)),
            pl.BlockSpec((chosen, tokens), lambda i: (0, 0)),
        ],
        out_shape=[
            jax.ShapeDtypeStruct((tokens, width), BF16),
            jax.ShapeDtypeStruct((chosen, tokens), BF16),
        ],
        scratch_shapes=[pltpu.VMEM((tokens, width), F32), pltpu.VMEM((experts, tokens), F32)],
        compiler_params=params(32),
        cost_estimate=cost(4 * experts * 9 * tokens * width, 4 * experts * 80 * LANES),
        name="combine_parts",
    )(recv, ranks, first, routes, weights)


def exchange(value):
    return lax.all_to_all(value, "expert", split_axis=0, concat_axis=0, tiled=True)


def half_kernel(half_ref, left_ref, right_ref, *refs):
    product = dot_rows(left_ref[...], right_ref[...])
    if len(refs) > 1 and refs[0].shape[1] == right_ref.shape[1]:
        product, refs = product + refs[0][...].astype(F32), refs[1:]
    width = right_ref.shape[1] // len(refs)
    for i, ref in enumerate(refs):
        ref[...] = product[:, i * width : (i + 1) * width].astype(BF16)


def half_product(half, left, right, tile, arrived=(), pieces=1):
    total, columns = left.shape
    width = right.shape[1]
    rows = columns // 2
    steps = rows // tile
    by_rows = lambda n: pl.BlockSpec((tile, n), lambda i, half: (i, 0))
    return pl.pallas_call(
        half_kernel,
        grid_spec=pltpu.PrefetchScalarGridSpec(
            num_scalar_prefetch=1,
            grid=(steps,),
            in_specs=[
                pl.BlockSpec((total, tile), lambda i, half: (0, half[0] * steps + i)),
                pl.BlockSpec(
                    right.shape, lambda i, half: (0, 0), pipeline_mode=pl.Buffered(1)
                ),
            ]
            + [by_rows(width) for _ in arrived],
            out_specs=[by_rows(width // pieces)] * pieces,
        ),
        out_shape=[jax.ShapeDtypeStruct((rows, width // pieces), BF16)] * pieces,
        compiler_params=params(60),
        cost_estimate=cost(2 * total * rows * width, 10 * MIB),
        name="half_product",
    )(half, left, right, *arrived)


def over_dp(value):
    return lax.ppermute(value, "dp", [(0, 1), (1, 0)])


def body(tokens, routes, router_weights, w_gate, w_up, w_down, out_grad):
    experts = lax.axis_size("expert")
    width = tokens.shape[1]
    gate, up, down = w_gate[0], w_up[0], w_down[0]
    routes, weights = routes.T, router_weights.T
    send, ranks = pack(0, experts, routes, weights, tokens, out_grad)
    recv = exchange(send)
    ranks, routes_b = lax.optimization_barrier((ranks, routes))
    send_2, _ = pack(1, experts, routes_b, weights, tokens, out_grad)
    recv_2 = exchange(send_2)
    send_back, *held, router = expert(0, recv, gate, up, down)
    recv_2, send_back = lax.optimization_barrier((recv_2, send_back))
    recv_back = exchange(send_back)
    send_back_2, x, dy, grads, hidden = expert(1, recv_2, gate, up, down, [router, *held])
    recv_back_2 = exchange(send_back_2)
    first = first_sum(recv_back, ranks, width)
    mine = lax.axis_index("dp").astype(jnp.int32).reshape(1)
    arrived = over_dp(half_product(1 - mine, x, grads, 256)[0])
    arrived_down = over_dp(half_product(1 - mine, hidden, dy, 128)[0])
    gate_grad, up_grad = half_product(mine, x, grads, 256, [arrived], 2)
    (down_grad,) = half_product(mine, hidden, dy, 128, [arrived_down])
    recv_back_2, gate_grad, up_grad, down_grad = lax.optimization_barrier(
        (recv_back_2, gate_grad, up_grad, down_grad)
    )
    tokens_grad, router_grad = combine(recv_back_2, ranks, first, routes, weights)
    return (tokens_grad, router_grad.T, gate_grad[None], up_grad[None], down_grad[None])


def solution(mesh):
    placed = (
        P(("dp", "expert"), None),
        P(("dp", "expert"), None),
        P(("dp", "expert"), None),
        P("expert", None, None),
        P("expert", None, None),
        P("expert", None, None),
        P(("dp", "expert"), None),
    )
    return jax.shard_map(
        body,
        mesh=mesh,
        in_specs=placed,
        out_specs=(
            P(("dp", "expert"), None),
            P(("dp", "expert"), None),
            P("expert", "dp", None),
            P("expert", "dp", None),
            P("expert", "dp", None),
        ),
        check_vma=False,
    )
```

```python
import functools

import jax
import jax.numpy as jnp
from jax import lax
from jax.experimental import pallas as pl
from jax.experimental.pallas import tpu as pltpu
from jax.sharding import PartitionSpec as P

F32, BF16 = jnp.float32, jnp.bfloat16
PARTS = 2
SLOTS = 8
GROUP = 16
MAIN = GROUP * SLOTS
ROWS = MAIN + GROUP
FINE = GROUP * 16
TILES = 9
STEP = 2
LANES = 128
MIB = 1 << 20


def iota(shape, axis):
    return lax.broadcasted_iota(jnp.int32, shape, axis)


def dot(a, b):
    return jnp.dot(a, b, preferred_element_type=F32)


def dot_columns(a, b):
    return lax.dot_general(a, b, (((1,), (1,)), ((), ())), preferred_element_type=F32)


def dot_rows(a, b):
    return lax.dot_general(a, b, (((0,), (0,)), ((), ())), preferred_element_type=F32)


def ones_where(mask):
    return jnp.where(mask, 1.0, 0.0).astype(BF16)


def unit(n, m):
    return ones_where(iota((n, m), 0) == iota((n, m), 1))


def spread_rows(block):
    wide = jnp.broadcast_to(block[:, None, :], (GROUP, 16, LANES))
    return wide.reshape(FINE, LANES)


def chunk_rows(value, pieces):
    width = value.shape[1] // pieces
    return jnp.concatenate([value[:, i * width : (i + 1) * width] for i in range(pieces)], axis=0)


def chunk_columns(value, pieces):
    height = value.shape[0] // pieces
    return jnp.concatenate([value[i * height : (i + 1) * height] for i in range(pieces)], axis=1)


def get_tiles(ref, group, first, count):
    here = slice(group * GROUP, (group + 1) * GROUP)
    return jnp.concatenate(
        [
            ref[here, j * 16 : (j + 1) * 16, :].reshape(FINE, LANES)
            for j in range(first, first + count)
        ],
        axis=1,
    )


def put_tiles(ref, group, first, value):
    here = slice(group * GROUP, (group + 1) * GROUP)
    for j in range(value.shape[1] // LANES):
        at = (first + j) * 16
        ref[here, at : at + 16, :] = value[:, j * LANES : (j + 1) * LANES].reshape(
            GROUP, 16, LANES
        )


def fine_of(pieces):
    row, col = iota((FINE, FINE), 0), iota((FINE, FINE), 1)
    s, q = row // 16, row % 16
    rows = 16 // pieces
    return ones_where(col == (q % pieces) * (FINE // pieces) + s * rows + q // pieces)


def rows_of(pieces):
    row, col = iota((FINE, FINE), 0), iota((FINE, FINE), 1)
    rows = 16 // pieces
    c, s, r = row // (FINE // pieces), (row // rows) % GROUP, row % rows
    return ones_where(col == s * 16 + r * pieces + c)


def unpack(ref, group, first):
    main = dot(rows_of(2), get_tiles(ref, group, first, TILES - 1)).astype(BF16)
    last = dot(rows_of(16), get_tiles(ref, group, first + TILES - 1, 1)).astype(BF16)
    return jnp.concatenate([chunk_columns(main, 2), chunk_columns(last, 16)], axis=0)


def repack(ref, group, first, rows):
    main = dot(fine_of(2), chunk_rows(rows[:MAIN], 2)).astype(BF16)
    last = dot(fine_of(16), chunk_rows(rows[MAIN:], 16)).astype(BF16)
    put_tiles(ref, group, first, main)
    put_tiles(ref, group, first + TILES - 1, last)


def route_tables(routes_ref, weights_ref, experts):
    chosen, tokens = routes_ref.shape
    expert = iota((experts, tokens), 0)
    mask = jnp.zeros((experts, tokens), F32)
    weight = jnp.zeros((experts, tokens), F32)
    for k in range(chosen):
        hit = routes_ref[k : k + 1, :] == expert
        mask = mask + jnp.where(hit, 1.0, 0.0)
        weight = weight + jnp.where(hit, weights_ref[k : k + 1, :].astype(F32), 0.0)
    earlier = ones_where(iota((tokens, tokens), 0) < iota((tokens, tokens), 1))
    return jnp.where(mask > 0.5, dot(mask.astype(BF16), earlier), -1.0), weight


def pack_kernel(part, routes_ref, weights_ref, x_ref, dy_ref, send_ref, ranks_ref, rank_ref, weight_ref):
    step = pl.program_id(0)

    @pl.when(step == 0)
    def _():
        rank_ref[...], weight_ref[...] = route_tables(routes_ref, weights_ref, rank_ref.shape[0])

    here = pl.ds(pl.multiple_of(step * GROUP, GROUP), GROUP)
    ranks_ref[...] = rank_ref[here, :]
    ranks, weights = rank_ref[here, :], weight_ref[here, :]
    wide, weight = spread_rows(ranks), spread_rows(weights)
    fine = iota((FINE, LANES), 0) % 16
    main = wide == (part * SLOTS + fine // 2).astype(F32)
    over = ranks == float(PARTS * SLOTS + part)
    for first, ref, value, single in ((0, x_ref, 1.0, 1.0), (TILES, dy_ref, weight, weights)):
        rows = ref[...]
        pick = jnp.concatenate(
            [jnp.where(main & (fine % 2 == c), value, 0.0).astype(BF16) for c in range(2)], axis=1
        )
        put_tiles(send_ref, 0, first, dot(pick, chunk_rows(rows, 2)).astype(BF16))
        last = dot(jnp.where(over, single, 0.0).astype(BF16), rows).astype(BF16)
        piece = dot(fine_of(16), chunk_rows(last, 16))
        put_tiles(send_ref, 0, first + TILES - 1, piece.astype(BF16))


def expert_kernel(part, recv_ref, gate_ref, up_ref, down_ref, *refs):
    outs = refs[-6:-1] if part == 0 else refs[-5:]
    send_ref, x_ref, dy_ref, grads_ref, sh_ref = outs
    units = gate_ref.shape[1]
    x = jnp.concatenate([unpack(recv_ref, i, 0) for i in range(STEP)], axis=0)
    dy = jnp.concatenate([unpack(recv_ref, i, TILES) for i in range(STEP)], axis=0)
    x_ref[...] = x
    dy_ref[...] = dy
    pre_gate = dot(x, gate_ref[...])
    pre_up = dot(x, up_ref[...])
    back = dot_columns(dy, down_ref[...])
    sig = jax.nn.sigmoid(pre_gate)
    active = pre_gate * sig
    hidden = active * pre_up
    sh_ref[...] = hidden.astype(BF16)
    router = jnp.sum(back * hidden, axis=1, keepdims=True)
    gate_grads = (back * pre_up * sig * (1.0 + pre_gate * (1.0 - sig))).astype(BF16)
    up_grads = (back * active).astype(BF16)
    grads_ref[:, :units] = gate_grads
    grads_ref[:, units:] = up_grads
    token_part = dot_columns(gate_grads, gate_ref[...]) + dot_columns(up_grads, up_ref[...])
    token_part = token_part.astype(BF16)
    router = jnp.broadcast_to(router, (STEP * ROWS, LANES)).astype(BF16)
    if part == 0:
        refs[-1][...] = router
    for i in range(STEP):
        rows = slice(i * ROWS, (i + 1) * ROWS)
        repack(send_ref, i, 0, token_part[rows])
        if part == 1:
            both_parts = jnp.concatenate([refs[0][rows, :], router[rows]], axis=0)
            shape = (FINE, PARTS * ROWS)
            fine, col = iota(shape, 0), iota(shape, 1)
            s, q = fine // 16, fine % 16
            main = ones_where(col == (q // SLOTS) * ROWS + s * SLOTS + q % SLOTS)
            over = ones_where((q < PARTS) & (col == q * ROWS + MAIN + s))
            low = iota((FINE, LANES), 1) < LANES // 2
            tile = jnp.where(low, dot(main, both_parts), dot(over, both_parts))
            put_tiles(send_ref, i, TILES, tile.astype(BF16))


def add_rows(part, ref, ranks, total_ref):
    tokens = ranks.shape[1]
    across = ones_where(iota((GROUP, FINE), 0) == iota((GROUP, FINE), 1) // 16)
    by_token = dot_rows(ranks.astype(BF16), across)
    single = dot_rows(ranks.astype(BF16), unit(GROUP, GROUP))
    fine = iota((tokens, FINE), 1) % 16
    main = by_token == (part * SLOTS + fine // 2).astype(F32)
    tiles = get_tiles(ref, 0, 0, TILES - 1)
    half = [dot(ones_where(main & (fine % 2 == c)), tiles) for c in range(2)]
    last = dot(rows_of(16), get_tiles(ref, 0, TILES - 1, 1)).astype(BF16)
    over = ones_where(single == float(PARTS * SLOTS + part))
    total_ref[...] += jnp.concatenate(half, axis=1) + dot(over, chunk_columns(last, 16))


def first_sum_kernel(recv_ref, rank_ref, total_ref):
    @pl.when(pl.program_id(0) == 0)
    def _():
        total_ref[...] = jnp.zeros_like(total_ref)

    add_rows(0, recv_ref, rank_ref[...], total_ref)


def combine_kernel(
    recv_ref, rank_ref, first_ref, routes_ref, weights_ref, grad_ref, router_ref, total_ref, value_ref
):
    step = pl.program_id(0)
    chosen, tokens = routes_ref.shape

    @pl.when(step == 0)
    def _():
        total_ref[...] = first_ref[...]

    ranks = rank_ref[...]
    add_rows(1, recv_ref, ranks, total_ref)
    wide = spread_rows(ranks)
    place = iota((FINE, LANES), 0) % 16
    tile = get_tiles(recv_ref, 0, TILES, 1).astype(F32)
    middle = LANES // 2
    value = jnp.where(wide == place.astype(F32), tile[:, 0:1], 0.0) + jnp.where(
        wide == (PARTS * SLOTS + place).astype(F32), tile[:, middle : middle + 1], 0.0
    )
    here = pl.ds(pl.multiple_of(step * GROUP, GROUP), GROUP)
    value_ref[here, :] = jnp.sum(value.reshape(GROUP, 16, LANES), axis=1)

    @pl.when(step == pl.num_programs(0) - 1)
    def _():
        grad_ref[...] = total_ref[...].astype(BF16)
        expert = iota(value_ref.shape, 0)
        row = iota((chosen, tokens), 0)
        out = jnp.zeros((chosen, tokens), F32)
        for k in range(chosen):
            picked = jnp.where(routes_ref[k : k + 1, :] == expert, value_ref[...], 0.0)
            out = jnp.where(row == k, jnp.sum(picked, axis=0, keepdims=True), out)
        router_ref[...] = (out / weights_ref[...].astype(F32)).astype(BF16)


def whole(shape):
    return pl.BlockSpec(shape, lambda i: (0,) * len(shape), pipeline_mode=pl.Buffered(1))


def params(mib):
    return pltpu.CompilerParams(vmem_limit_bytes=mib * MIB, dimension_semantics=("arbitrary",))


def cost(flops, size):
    return pl.CostEstimate(flops=flops, bytes_accessed=size, transcendentals=0)


def by_group(size, high):
    return pl.BlockSpec((size, high, LANES), lambda i: (i, 0, 0))


def pack(part, experts, routes, weights, x, dy):
    tokens, width = x.shape
    high = 2 * TILES * 16
    return pl.pallas_call(
        functools.partial(pack_kernel, part),
        grid=(experts // GROUP,),
        in_specs=[whole(routes.shape), whole(weights.shape), whole(x.shape), whole(dy.shape)],
        out_specs=[by_group(GROUP, high), pl.BlockSpec((GROUP, tokens), lambda i: (i, 0))],
        out_shape=[
            jax.ShapeDtypeStruct((experts, high, LANES), BF16),
            jax.ShapeDtypeStruct((experts, tokens), F32),
        ],
        scratch_shapes=[pltpu.VMEM((experts, tokens), F32)] * 2,
        compiler_params=params(60),
        cost_estimate=cost(8 * experts * 16 * tokens * width, 2 * experts * high * LANES),
        name="pack_rows",
    )(routes, weights, x, dy)


def expert(part, recv, gate, up, down, held=()):
    sources = recv.shape[0]
    width, units = gate.shape
    rows = sources // GROUP * ROWS
    steps = sources // (STEP * GROUP)
    high = (TILES + part) * 16
    by_rows = lambda n: pl.BlockSpec((STEP * ROWS, n), lambda i: (i + part * steps, 0))
    router = pl.BlockSpec((STEP * ROWS, LANES), lambda i: (i, 0))
    anywhere = pl.BlockSpec(memory_space=pl.ANY)
    return pl.pallas_call(
        functools.partial(expert_kernel, part),
        grid=(steps,),
        in_specs=[by_group(STEP * GROUP, recv.shape[1])]
        + [whole(w.shape) for w in (gate, up, down)]
        + ([router] + [anywhere] * 4 if part else []),
        out_specs=[by_group(STEP * GROUP, high)]
        + [by_rows(n) for n in (width, width, 2 * units, units)]
        + ([] if part else [router]),
        out_shape=[jax.ShapeDtypeStruct((sources, high, LANES), BF16)]
        + [
            jax.ShapeDtypeStruct((PARTS * rows, n), BF16) for n in (width, width, 2 * units, units)
        ]
        + ([] if part else [jax.ShapeDtypeStruct((rows, LANES), BF16)]),
        input_output_aliases={5 + i: 1 + i for i in range(4)} if part else {},
        compiler_params=params(60),
        cost_estimate=cost(10 * rows * width * units, 30 * MIB),
        name="expert",
    )(recv, gate, up, down, *held)


def first_sum(recv, ranks, width):
    experts, tokens = ranks.shape
    return pl.pallas_call(
        first_sum_kernel,
        grid=(experts // GROUP,),
        in_specs=[
            by_group(GROUP, recv.shape[1]),
            pl.BlockSpec((GROUP, tokens), lambda i: (i, 0)),
        ],
        out_specs=pl.BlockSpec((tokens, width), lambda i: (0, 0)),
        out_shape=jax.ShapeDtypeStruct((tokens, width), F32),
        compiler_params=params(60),
        cost_estimate=cost(4 * experts * 9 * tokens * width, 4 * experts * 80 * LANES),
        name="first_sum",
    )(recv, ranks)


def combine(recv, ranks, first, routes, weights):
    experts = recv.shape[0]
    chosen, tokens = routes.shape
    width = first.shape[1]
    return pl.pallas_call(
        combine_kernel,
        grid=(experts // GROUP,),
        in_specs=[
            by_group(GROUP, recv.shape[1]),
            pl.BlockSpec((GROUP, tokens), lambda i: (i, 0)),
            whole(first.shape),
            whole(routes.shape),
            whole(weights.shape),
        ],
        out_specs=[
            pl.BlockSpec((tokens, width), lambda i: (0, 0)),
            pl.BlockSpec((chosen, tokens), lambda i: (0, 0)),
        ],
        out_shape=[
            jax.ShapeDtypeStruct((tokens, width), BF16),
            jax.ShapeDtypeStruct((chosen, tokens), BF16),
        ],
        scratch_shapes=[pltpu.VMEM((tokens, width), F32), pltpu.VMEM((experts, tokens), F32)],
        compiler_params=params(60),
        cost_estimate=cost(4 * experts * 9 * tokens * width, 4 * experts * 80 * LANES),
        name="combine_parts",
    )(recv, ranks, first, routes, weights)


def exchange(value):
    return lax.all_to_all(value, "expert", split_axis=0, concat_axis=0, tiled=True)


def half_kernel(half_ref, left_ref, right_ref, *refs):
    product = dot_rows(left_ref[...], right_ref[...])
    if len(refs) > 1 and refs[0].shape[1] == right_ref.shape[1]:
        product, refs = product + refs[0][...].astype(F32), refs[1:]
    width = right_ref.shape[1] // len(refs)
    for i, ref in enumerate(refs):
        ref[...] = product[:, i * width : (i + 1) * width].astype(BF16)


def half_product(half, left, right, tile, arrived=(), pieces=1):
    total, columns = left.shape
    width = right.shape[1]
    rows = columns // 2
    steps = rows // tile
    by_rows = lambda n: pl.BlockSpec((tile, n), lambda i, half: (i, 0))
    return pl.pallas_call(
        half_kernel,
        grid_spec=pltpu.PrefetchScalarGridSpec(
            num_scalar_prefetch=1,
            grid=(steps,),
            in_specs=[
                pl.BlockSpec((total, tile), lambda i, half: (0, half[0] * steps + i)),
                pl.BlockSpec(
                    right.shape, lambda i, half: (0, 0), pipeline_mode=pl.Buffered(1)
                ),
            ]
            + [by_rows(width) for _ in arrived],
            out_specs=[by_rows(width // pieces)] * pieces,
        ),
        out_shape=[jax.ShapeDtypeStruct((rows, width // pieces), BF16)] * pieces,
        compiler_params=params(60),
        cost_estimate=cost(2 * total * rows * width, 10 * MIB),
        name="half_product",
    )(half, left, right, *arrived)


def over_dp(value):
    return lax.ppermute(value, "dp", [(0, 1), (1, 0)])


def body(tokens, routes, router_weights, w_gate, w_up, w_down, out_grad):
    experts = lax.axis_size("expert")
    width = tokens.shape[1]
    gate, up, down = w_gate[0], w_up[0], w_down[0]
    routes, weights = routes.T, router_weights.T
    send, ranks = pack(0, experts, routes, weights, tokens, out_grad)
    recv = exchange(send)
    ranks, routes_b = lax.optimization_barrier((ranks, routes))
    send_2, _ = pack(1, experts, routes_b, weights, tokens, out_grad)
    recv_2 = exchange(send_2)
    send_back, *held, router = expert(0, recv, gate, up, down)
    recv_2, send_back = lax.optimization_barrier((recv_2, send_back))
    recv_back = exchange(send_back)
    send_back_2, x, dy, grads, hidden = expert(1, recv_2, gate, up, down, [router, *held])
    recv_back_2 = exchange(send_back_2)
    first = first_sum(recv_back, ranks, width)
    mine = lax.axis_index("dp").astype(jnp.int32).reshape(1)
    arrived = over_dp(half_product(1 - mine, x, grads, 256)[0])
    arrived_down = over_dp(half_product(1 - mine, hidden, dy, 128)[0])
    gate_grad, up_grad = half_product(mine, x, grads, 256, [arrived], 2)
    (down_grad,) = half_product(mine, hidden, dy, 128, [arrived_down])
    recv_back_2, gate_grad, up_grad, down_grad = lax.optimization_barrier(
        (recv_back_2, gate_grad, up_grad, down_grad)
    )
    tokens_grad, router_grad = combine(recv_back_2, ranks, first, routes, weights)
    return (tokens_grad, router_grad.T, gate_grad[None], up_grad[None], down_grad[None])


def solution(mesh):
    placed = (
        P(("dp", "expert"), None),
        P(("dp", "expert"), None),
        P(("dp", "expert"), None),
        P("expert", None, None),
        P("expert", None, None),
        P("expert", None, None),
        P(("dp", "expert"), None),
    )
    return jax.shard_map(
        body,
        mesh=mesh,
        in_specs=placed,
        out_specs=(
            P(("dp", "expert"), None),
            P(("dp", "expert"), None),
            P("expert", "dp", None),
            P("expert", "dp", None),
            P("expert", "dp", None),
        ),
        check_vma=False,
    )
```

```python
import functools

import jax
import jax.numpy as jnp
from jax import lax
from jax.experimental import pallas as pl
from jax.experimental.pallas import tpu as pltpu
from jax.sharding import PartitionSpec as P

F32, BF16 = jnp.float32, jnp.bfloat16
PARTS = 2
SLOTS = 8
GROUP = 16
MAIN = GROUP * SLOTS
ROWS = MAIN + GROUP
FINE = GROUP * 16
TILES = 9
STEP = 2
LANES = 128
MIB = 1 << 20


def iota(shape, axis):
    return lax.broadcasted_iota(jnp.int32, shape, axis)


def dot(a, b):
    return jnp.dot(a, b, preferred_element_type=F32)


def dot_columns(a, b):
    return lax.dot_general(a, b, (((1,), (1,)), ((), ())), preferred_element_type=F32)


def dot_rows(a, b):
    return lax.dot_general(a, b, (((0,), (0,)), ((), ())), preferred_element_type=F32)


def ones_where(mask):
    return jnp.where(mask, 1.0, 0.0).astype(BF16)


def unit(n, m):
    return ones_where(iota((n, m), 0) == iota((n, m), 1))


def spread_rows(block):
    wide = jnp.broadcast_to(block[:, None, :], (GROUP, 16, LANES))
    return wide.reshape(FINE, LANES)


def chunk_rows(value, pieces):
    width = value.shape[1] // pieces
    return jnp.concatenate([value[:, i * width : (i + 1) * width] for i in range(pieces)], axis=0)


def chunk_columns(value, pieces):
    height = value.shape[0] // pieces
    return jnp.concatenate([value[i * height : (i + 1) * height] for i in range(pieces)], axis=1)


def get_tiles(ref, group, first, count):
    here = slice(group * GROUP, (group + 1) * GROUP)
    return jnp.concatenate(
        [
            ref[here, j * 16 : (j + 1) * 16, :].reshape(FINE, LANES)
            for j in range(first, first + count)
        ],
        axis=1,
    )


def put_tiles(ref, group, first, value):
    here = slice(group * GROUP, (group + 1) * GROUP)
    for j in range(value.shape[1] // LANES):
        at = (first + j) * 16
        ref[here, at : at + 16, :] = value[:, j * LANES : (j + 1) * LANES].reshape(
            GROUP, 16, LANES
        )


def fine_of(pieces):
    row, col = iota((FINE, FINE), 0), iota((FINE, FINE), 1)
    s, q = row // 16, row % 16
    rows = 16 // pieces
    return ones_where(col == (q % pieces) * (FINE // pieces) + s * rows + q // pieces)


def rows_of(pieces):
    row, col = iota((FINE, FINE), 0), iota((FINE, FINE), 1)
    rows = 16 // pieces
    c, s, r = row // (FINE // pieces), (row // rows) % GROUP, row % rows
    return ones_where(col == s * 16 + r * pieces + c)


def unpack(ref, group, first):
    main = dot(rows_of(2), get_tiles(ref, group, first, TILES - 1)).astype(BF16)
    last = dot(rows_of(16), get_tiles(ref, group, first + TILES - 1, 1)).astype(BF16)
    return jnp.concatenate([chunk_columns(main, 2), chunk_columns(last, 16)], axis=0)


def repack(ref, group, first, rows):
    main = dot(fine_of(2), chunk_rows(rows[:MAIN], 2)).astype(BF16)
    last = dot(fine_of(16), chunk_rows(rows[MAIN:], 16)).astype(BF16)
    put_tiles(ref, group, first, main)
    put_tiles(ref, group, first + TILES - 1, last)


def route_tables(routes_ref, weights_ref, experts):
    chosen, tokens = routes_ref.shape
    expert = iota((experts, tokens), 0)
    mask = jnp.zeros((experts, tokens), F32)
    weight = jnp.zeros((experts, tokens), F32)
    for k in range(chosen):
        hit = routes_ref[k : k + 1, :] == expert
        mask = mask + jnp.where(hit, 1.0, 0.0)
        weight = weight + jnp.where(hit, weights_ref[k : k + 1, :].astype(F32), 0.0)
    earlier = ones_where(iota((tokens, tokens), 0) < iota((tokens, tokens), 1))
    return jnp.where(mask > 0.5, dot(mask.astype(BF16), earlier), -1.0), weight


def pack_kernel(part, routes_ref, weights_ref, x_ref, dy_ref, send_ref, ranks_ref, rank_ref, weight_ref):
    step = pl.program_id(0)

    @pl.when(step == 0)
    def _():
        rank_ref[...], weight_ref[...] = route_tables(routes_ref, weights_ref, rank_ref.shape[0])

    here = pl.ds(pl.multiple_of(step * GROUP, GROUP), GROUP)
    ranks_ref[...] = rank_ref[here, :]
    ranks, weights = rank_ref[here, :], weight_ref[here, :]
    wide, weight = spread_rows(ranks), spread_rows(weights)
    fine = iota((FINE, LANES), 0) % 16
    main = wide == (part * SLOTS + fine // 2).astype(F32)
    over = ranks == float(PARTS * SLOTS + part)
    for first, ref, value, single in ((0, x_ref, 1.0, 1.0), (TILES, dy_ref, weight, weights)):
        rows = ref[...]
        pick = jnp.concatenate(
            [jnp.where(main & (fine % 2 == c), value, 0.0).astype(BF16) for c in range(2)], axis=1
        )
        put_tiles(send_ref, 0, first, dot(pick, chunk_rows(rows, 2)).astype(BF16))
        last = dot(jnp.where(over, single, 0.0).astype(BF16), rows).astype(BF16)
        piece = dot(fine_of(16), chunk_rows(last, 16))
        put_tiles(send_ref, 0, first + TILES - 1, piece.astype(BF16))


def expert_kernel(part, recv_ref, gate_ref, up_ref, down_ref, *refs):
    outs = refs[-6:-1] if part == 0 else refs[-5:]
    send_ref, x_ref, dy_ref, grads_ref, sh_ref = outs
    units = gate_ref.shape[1]
    x = jnp.concatenate([unpack(recv_ref, i, 0) for i in range(STEP)], axis=0)
    dy = jnp.concatenate([unpack(recv_ref, i, TILES) for i in range(STEP)], axis=0)
    x_ref[...] = x
    dy_ref[...] = dy
    pre_gate = dot(x, gate_ref[...])
    pre_up = dot(x, up_ref[...])
    back = dot_columns(dy, down_ref[...])
    sig = jax.nn.sigmoid(pre_gate)
    active = pre_gate * sig
    hidden = active * pre_up
    sh_ref[...] = hidden.astype(BF16)
    router = jnp.sum(back * hidden, axis=1, keepdims=True)
    gate_grads = (back * pre_up * sig * (1.0 + pre_gate * (1.0 - sig))).astype(BF16)
    up_grads = (back * active).astype(BF16)
    grads_ref[:, :units] = gate_grads
    grads_ref[:, units:] = up_grads
    token_part = dot_columns(gate_grads, gate_ref[...]) + dot_columns(up_grads, up_ref[...])
    token_part = token_part.astype(BF16)
    router = jnp.broadcast_to(router, (STEP * ROWS, LANES)).astype(BF16)
    if part == 0:
        refs[-1][...] = router
    for i in range(STEP):
        rows = slice(i * ROWS, (i + 1) * ROWS)
        repack(send_ref, i, 0, token_part[rows])
        if part == 1:
            both_parts = jnp.concatenate([refs[0][rows, :], router[rows]], axis=0)
            shape = (FINE, PARTS * ROWS)
            fine, col = iota(shape, 0), iota(shape, 1)
            s, q = fine // 16, fine % 16
            main = ones_where(col == (q // SLOTS) * ROWS + s * SLOTS + q % SLOTS)
            over = ones_where((q < PARTS) & (col == q * ROWS + MAIN + s))
            low = iota((FINE, LANES), 1) < LANES // 2
            tile = jnp.where(low, dot(main, both_parts), dot(over, both_parts))
            put_tiles(send_ref, i, TILES, tile.astype(BF16))


def add_rows(part, ref, ranks, total_ref):
    tokens = ranks.shape[1]
    across = ones_where(iota((GROUP, FINE), 0) == iota((GROUP, FINE), 1) // 16)
    by_token = dot_rows(ranks.astype(BF16), across)
    single = dot_rows(ranks.astype(BF16), unit(GROUP, GROUP))
    fine = iota((tokens, FINE), 1) % 16
    main = by_token == (part * SLOTS + fine // 2).astype(F32)
    tiles = get_tiles(ref, 0, 0, TILES - 1)
    half = [dot(ones_where(main & (fine % 2 == c)), tiles) for c in range(2)]
    last = dot(rows_of(16), get_tiles(ref, 0, TILES - 1, 1)).astype(BF16)
    over = ones_where(single == float(PARTS * SLOTS + part))
    total_ref[...] += jnp.concatenate(half, axis=1) + dot(over, chunk_columns(last, 16))


def first_sum_kernel(recv_ref, rank_ref, total_ref):
    @pl.when(pl.program_id(0) == 0)
    def _():
        total_ref[...] = jnp.zeros_like(total_ref)

    add_rows(0, recv_ref, rank_ref[...], total_ref)


def combine_kernel(
    recv_ref,
    rank_ref,
    first_hbm,
    routes_ref,
    weights_ref,
    grad_ref,
    router_ref,
    total_ref,
    value_ref,
    first_ref,
    copied,
):
    step = pl.program_id(0)
    copy = pltpu.make_async_copy(first_hbm, first_ref, copied)
    chosen, tokens = routes_ref.shape

    @pl.when(step == 0)
    def _():
        copy.start()
        total_ref[...] = jnp.zeros_like(total_ref)

    ranks = rank_ref[...]
    add_rows(1, recv_ref, ranks, total_ref)
    wide = spread_rows(ranks)
    place = iota((FINE, LANES), 0) % 16
    tile = get_tiles(recv_ref, 0, TILES, 1).astype(F32)
    middle = LANES // 2
    value = jnp.where(wide == place.astype(F32), tile[:, 0:1], 0.0) + jnp.where(
        wide == (PARTS * SLOTS + place).astype(F32), tile[:, middle : middle + 1], 0.0
    )
    here = pl.ds(pl.multiple_of(step * GROUP, GROUP), GROUP)
    value_ref[here, :] = jnp.sum(value.reshape(GROUP, 16, LANES), axis=1)

    @pl.when(step == pl.num_programs(0) - 1)
    def _():
        copy.wait()
        grad_ref[...] = (total_ref[...] + first_ref[...]).astype(BF16)
        expert = iota(value_ref.shape, 0)
        row = iota((chosen, tokens), 0)
        out = jnp.zeros((chosen, tokens), F32)
        for k in range(chosen):
            picked = jnp.where(routes_ref[k : k + 1, :] == expert, value_ref[...], 0.0)
            out = jnp.where(row == k, jnp.sum(picked, axis=0, keepdims=True), out)
        router_ref[...] = (out / weights_ref[...].astype(F32)).astype(BF16)


def whole(shape):
    return pl.BlockSpec(shape, lambda i: (0,) * len(shape), pipeline_mode=pl.Buffered(1))


def params(mib):
    return pltpu.CompilerParams(vmem_limit_bytes=mib * MIB, dimension_semantics=("arbitrary",))


def cost(flops, size):
    return pl.CostEstimate(flops=flops, bytes_accessed=size, transcendentals=0)


def by_group(size, high):
    return pl.BlockSpec((size, high, LANES), lambda i: (i, 0, 0))


def pack(part, experts, routes, weights, x, dy):
    tokens, width = x.shape
    high = 2 * TILES * 16
    return pl.pallas_call(
        functools.partial(pack_kernel, part),
        grid=(experts // GROUP,),
        in_specs=[whole(routes.shape), whole(weights.shape), whole(x.shape), whole(dy.shape)],
        out_specs=[by_group(GROUP, high), pl.BlockSpec((GROUP, tokens), lambda i: (i, 0))],
        out_shape=[
            jax.ShapeDtypeStruct((experts, high, LANES), BF16),
            jax.ShapeDtypeStruct((experts, tokens), F32),
        ],
        scratch_shapes=[pltpu.VMEM((experts, tokens), F32)] * 2,
        compiler_params=params(60),
        cost_estimate=cost(8 * experts * 16 * tokens * width, 2 * experts * high * LANES),
        name="pack_rows",
    )(routes, weights, x, dy)


def expert(part, recv, gate, up, down, held=()):
    sources = recv.shape[0]
    width, units = gate.shape
    rows = sources // GROUP * ROWS
    steps = sources // (STEP * GROUP)
    high = (TILES + part) * 16
    by_rows = lambda n: pl.BlockSpec((STEP * ROWS, n), lambda i: (i + part * steps, 0))
    router = pl.BlockSpec((STEP * ROWS, LANES), lambda i: (i, 0))
    anywhere = pl.BlockSpec(memory_space=pl.ANY)
    return pl.pallas_call(
        functools.partial(expert_kernel, part),
        grid=(steps,),
        in_specs=[by_group(STEP * GROUP, recv.shape[1])]
        + [whole(w.shape) for w in (gate, up, down)]
        + ([router] + [anywhere] * 4 if part else []),
        out_specs=[by_group(STEP * GROUP, high)]
        + [by_rows(n) for n in (width, width, 2 * units, units)]
        + ([] if part else [router]),
        out_shape=[jax.ShapeDtypeStruct((sources, high, LANES), BF16)]
        + [
            jax.ShapeDtypeStruct((PARTS * rows, n), BF16) for n in (width, width, 2 * units, units)
        ]
        + ([] if part else [jax.ShapeDtypeStruct((rows, LANES), BF16)]),
        input_output_aliases={5 + i: 1 + i for i in range(4)} if part else {},
        compiler_params=params(60),
        cost_estimate=cost(10 * rows * width * units, 30 * MIB),
        name="expert",
    )(recv, gate, up, down, *held)


def first_sum(recv, ranks, width):
    experts, tokens = ranks.shape
    return pl.pallas_call(
        first_sum_kernel,
        grid=(experts // GROUP,),
        in_specs=[
            by_group(GROUP, recv.shape[1]),
            pl.BlockSpec((GROUP, tokens), lambda i: (i, 0)),
        ],
        out_specs=pl.BlockSpec((tokens, width), lambda i: (0, 0)),
        out_shape=jax.ShapeDtypeStruct((tokens, width), F32),
        compiler_params=params(32),
        cost_estimate=cost(4 * experts * 9 * tokens * width, 4 * experts * 80 * LANES),
        name="first_sum",
    )(recv, ranks)


def combine(recv, ranks, first, routes, weights):
    experts = recv.shape[0]
    chosen, tokens = routes.shape
    width = first.shape[1]
    return pl.pallas_call(
        combine_kernel,
        grid=(experts // GROUP,),
        in_specs=[
            by_group(GROUP, recv.shape[1]),
            pl.BlockSpec((GROUP, tokens), lambda i: (i, 0)),
            pl.BlockSpec(memory_space=pltpu.HBM),
            whole(routes.shape),
            whole(weights.shape),
        ],
        out_specs=[
            pl.BlockSpec((tokens, width), lambda i: (0, 0)),
            pl.BlockSpec((chosen, tokens), lambda i: (0, 0)),
        ],
        out_shape=[
            jax.ShapeDtypeStruct((tokens, width), BF16),
            jax.ShapeDtypeStruct((chosen, tokens), BF16),
        ],
        scratch_shapes=[
            pltpu.VMEM((tokens, width), F32),
            pltpu.VMEM((experts, tokens), F32),
            pltpu.VMEM((tokens, width), F32),
            pltpu.SemaphoreType.DMA,
        ],
        compiler_params=params(32),
        cost_estimate=cost(4 * experts * 9 * tokens * width, 4 * experts * 80 * LANES),
        name="combine_parts",
    )(recv, ranks, first, routes, weights)


def exchange(value):
    return lax.all_to_all(value, "expert", split_axis=0, concat_axis=0, tiled=True)


def half_kernel(half_ref, left_ref, right_ref, *refs):
    product = dot_rows(left_ref[...], right_ref[...])
    if len(refs) > 1 and refs[0].shape[1] == right_ref.shape[1]:
        product, refs = product + refs[0][...].astype(F32), refs[1:]
    width = right_ref.shape[1] // len(refs)
    for i, ref in enumerate(refs):
        ref[...] = product[:, i * width : (i + 1) * width].astype(BF16)


def half_product(half, left, right, tile, arrived=(), pieces=1):
    total, columns = left.shape
    width = right.shape[1]
    rows = columns // 2
    steps = rows // tile
    by_rows = lambda n: pl.BlockSpec((tile, n), lambda i, half: (i, 0))
    return pl.pallas_call(
        half_kernel,
        grid_spec=pltpu.PrefetchScalarGridSpec(
            num_scalar_prefetch=1,
            grid=(steps,),
            in_specs=[
                pl.BlockSpec((total, tile), lambda i, half: (0, half[0] * steps + i)),
                pl.BlockSpec(
                    right.shape, lambda i, half: (0, 0), pipeline_mode=pl.Buffered(1)
                ),
            ]
            + [by_rows(width) for _ in arrived],
            out_specs=[by_rows(width // pieces)] * pieces,
        ),
        out_shape=[jax.ShapeDtypeStruct((rows, width // pieces), BF16)] * pieces,
        compiler_params=params(60),
        cost_estimate=cost(2 * total * rows * width, 10 * MIB),
        name="half_product",
    )(half, left, right, *arrived)


def over_dp(value):
    return lax.ppermute(value, "dp", [(0, 1), (1, 0)])


def body(tokens, routes, router_weights, w_gate, w_up, w_down, out_grad):
    experts = lax.axis_size("expert")
    width = tokens.shape[1]
    gate, up, down = w_gate[0], w_up[0], w_down[0]
    routes, weights = routes.T, router_weights.T
    send, ranks = pack(0, experts, routes, weights, tokens, out_grad)
    recv = exchange(send)
    ranks, routes_b = lax.optimization_barrier((ranks, routes))
    send_2, _ = pack(1, experts, routes_b, weights, tokens, out_grad)
    recv_2 = exchange(send_2)
    send_back, *held, router = expert(0, recv, gate, up, down)
    recv_2, send_back = lax.optimization_barrier((recv_2, send_back))
    recv_back = exchange(send_back)
    send_back_2, x, dy, grads, hidden = expert(1, recv_2, gate, up, down, [router, *held])
    recv_back_2 = exchange(send_back_2)
    first = first_sum(recv_back, ranks, width)
    mine = lax.axis_index("dp").astype(jnp.int32).reshape(1)
    arrived = over_dp(half_product(1 - mine, x, grads, 256)[0])
    arrived_down = over_dp(half_product(1 - mine, hidden, dy, 128)[0])
    gate_grad, up_grad = half_product(mine, x, grads, 256, [arrived], 2)
    (down_grad,) = half_product(mine, hidden, dy, 128, [arrived_down])
    recv_back_2, gate_grad, up_grad, down_grad = lax.optimization_barrier(
        (recv_back_2, gate_grad, up_grad, down_grad)
    )
    tokens_grad, router_grad = combine(recv_back_2, ranks, first, routes, weights)
    return (tokens_grad, router_grad.T, gate_grad[None], up_grad[None], down_grad[None])


def solution(mesh):
    placed = (
        P(("dp", "expert"), None),
        P(("dp", "expert"), None),
        P(("dp", "expert"), None),
        P("expert", None, None),
        P("expert", None, None),
        P("expert", None, None),
        P(("dp", "expert"), None),
    )
    return jax.shard_map(
        body,
        mesh=mesh,
        in_specs=placed,
        out_specs=(
            P(("dp", "expert"), None),
            P(("dp", "expert"), None),
            P("expert", "dp", None),
            P("expert", "dp", None),
            P("expert", "dp", None),
        ),
        check_vma=False,
    )
```
